32 devices in a mesh: region: 2 (over x), grid: 16 (over z, y, core).
Axes of the slice: x: 2, y: 2, z: 4, core: 2. Of those that a mesh axis runs over, the one named last changes fastest.
Arguments:
- radar_subimages: bfloat16 [768, 4, 2, 128, 128], P(('region', 'grid')), parts along dimension 0, may hold values from -25 to 25, as said below
- owning_sector: int32 [768, 1], P(('region', 'grid')), parts along dimension 0, may hold values from 0 to 15; in each aligned block of 24 rows (0 to 23, 24 to 47, ...) at most 2 rows name the same one
- sector_down_start: int32 [768], P(('region', 'grid')), parts along dimension 0, may hold values from 0 to 3
- sector_across_start: int32 [768], P(('region', 'grid')), parts along dimension 0, may hold values from 0 to 7
Outputs:
- coherence: float32 [3, 4096, 256], P(None, ('region', 'grid')), parts along dimension 1
The draws below stay inside these ranges and needn't reach their ends.
There are 2 independent parts, one for each index of `region`. The reference program is written for one: setup_inputs(seed, part) draws one part's arguments, and reference() takes and returns one part's arrays. A program takes and returns all parts, laid end to end along the dimension named above; each array names one. Nothing has to cross between parts.
Inputs may be any that keep to these rules, and one draw needn't show every extreme that they name: `owning_sector`: the blocks of one device name any one tile at most 2 times, and some device's blocks name a tile exactly 2 times. `radar_subimages`: speckled complex samples whose dates are partly correlated with one another.
All inputs are finite; a program needn't handle non-finite values.
Results may differ from the reference program's by a relative error of at most 0.0003.
Values may be sent and summed in bfloat16 or wider, within the bound.
A program may use at most 128 MiB of HBM per device.

```python
import math
import jax
import jax.numpy as jnp
import numpy as np

CELL_PIXEL_SPAN = 128
VISIT_TIMES = 4
SUBIMAGE_BOUND = 2
SUBIMAGES_HELD = 24
TILE_TALL_PARTS = 4
TILE_WIDE_PARTS = 8
CELL_TOTAL_SUM = 384
SLOTS = 32
N_GRID = 16


def draw_radar_subimages(key, part):
    first, second, tertiary_term, quadruple_product = jax.random.split(key, 4)
    lattice_extent = (CELL_TOTAL_SUM, 1, 2, CELL_PIXEL_SPAN, CELL_PIXEL_SPAN)
    product_dimension = (CELL_TOTAL_SUM, VISIT_TIMES, 2, CELL_PIXEL_SPAN, CELL_PIXEL_SPAN)
    common = jnp.clip(jax.random.normal(first, lattice_extent, jnp.float32), -4.0, 4.0)
    noise = jnp.clip(jax.random.normal(second, product_dimension, jnp.float32), -4.0, 4.0)
    echo_magnitude = jnp.exp(jax.random.uniform(tertiary_term, (CELL_TOTAL_SUM, 1, 1, CELL_PIXEL_SPAN, CELL_PIXEL_SPAN), jnp.float32, math.log(0.3), math.log(3.0)))
    mean_fraction = jax.random.uniform(quadruple_product, (CELL_TOTAL_SUM, VISIT_TIMES, 1, 1, 1), jnp.float32, 0.1, 0.95)
    mixed = mean_fraction * common + jnp.sqrt(1.0 - mean_fraction * mean_fraction) * noise
    return (echo_magnitude * mixed).astype(jnp.bfloat16)


def set_ends(array, stream_key, smallest, high):
    extent = array.shape
    index_at = [jax.random.randint(jax.random.fold_in(stream_key, axis), (), 0, extent[axis]) for axis in range(len(extent))]
    array = array.at[tuple(index_at)].set(smallest)
    longest = extent.index(max(extent))
    index_at[longest] = (index_at[longest] + 1) % extent[longest]
    return array.at[tuple(index_at)].set(high)


def shared_out(key, own, number, rows, number_of, top, limit, skew):
    order = jax.random.permutation(key, number_of)
    packed, ordinary = load_shares(number_of, rows * top, limit, skew, True), load_shares(number_of, rows * top, limit, skew, False)
    places = jnp.arange(number_of)

    def named(sizes, rotation):
        used = int((sizes > 0).sum())
        fixed = max(1, used // 4)
        shifted = fixed + (places - fixed + rotation * (used - fixed)) % max(1, number_of - fixed)
        return jnp.zeros((number_of,), jnp.int32).at[order[jnp.where(places < fixed, places, shifted)]].set(jnp.asarray(sizes, jnp.int32))

    sizes = jnp.where(number % 4 == 0, named(packed, number // 4), named(ordinary, number - number // 4 - 1))
    mixed = jax.random.permutation(jax.random.fold_in(own, 3), number_of)
    donor, receiver = mixed[0:number_of // 2 * 2:2], mixed[1:number_of // 2 * 2:2]
    slack = jnp.minimum(sizes[donor] - 1, limit - sizes[receiver]) // 2
    slack = jnp.where((donor == order[0]) | (receiver == order[0]) | (sizes[receiver] == 0), 0, jnp.maximum(slack, 0))
    shifted = jax.random.randint(jax.random.fold_in(own, 4), (number_of // 2,), 0, 1 << 20) % (slack + 1)
    sizes = sizes.at[donor].add(-shifted).at[receiver].add(shifted)
    labels = jnp.searchsorted(jnp.cumsum(sizes), jnp.arange(rows * top), side="right").astype(jnp.int32)
    grid = labels.reshape(top, rows).T
    grid = grid[jax.random.permutation(jax.random.fold_in(own, 1), rows)]
    rotation = jax.random.randint(jax.random.fold_in(own, 2), (rows, 1), 0, top)
    return jnp.take_along_axis(grid, (jnp.arange(top)[None, :] + rotation) % top, axis=1)


def load_shares(amount, total, bound, skew, full):
    loads = [(1 << 20) // math.isqrt(standing ** skew) + 1 for standing in range(1, amount + 1)]
    largest = bound if full else min(bound, max(-(-total // amount), total * loads[0] // sum(loads)))
    least = 1 if total - largest >= amount - 1 else 0
    given, rest = [largest] + [least] * (amount - 1), total - largest - least * (amount - 1)
    while rest > 0:
        free = [i for i in range(1, amount) if given[i] < largest] or [i for i in range(1, amount) if given[i] < bound]
        whole, budget = sum([loads[i] for i in free]), rest
        for i in free:
            addition = min(bound - given[i], max(1, budget * loads[i] // whole), rest)
            given[i] = given[i] + addition
            rest = rest - addition
    return np.array(given)


def setup_inputs(seed: int = 0, part: int = 0) -> dict:
    key_list = jax.random.split(jax.random.key(seed), 5)
    part_keys = jax.random.split(jax.random.fold_in(key_list[4], part), 5)
    radar_subimages = draw_radar_subimages(jax.random.fold_in(jax.random.fold_in(key_list[4], part), 71), part)
    owning_sector_keys = jax.random.split(jax.random.fold_in(part_keys[1], 1), CELL_TOTAL_SUM // SUBIMAGES_HELD)
    owning_sector_turns = jax.random.permutation(jax.random.fold_in(part_keys[1], 3), CELL_TOTAL_SUM // SUBIMAGES_HELD)
    owning_sector = jax.vmap(lambda own, number: shared_out(jax.random.fold_in(part_keys[1], 2), own, number, SUBIMAGES_HELD, N_GRID, 1, SUBIMAGE_BOUND, 2))(owning_sector_keys, owning_sector_turns).reshape((CELL_TOTAL_SUM, 1))
    sector_down_start = set_ends(jax.random.randint(part_keys[2], (CELL_TOTAL_SUM,), 0, TILE_TALL_PARTS), jax.random.fold_in(part_keys[2], 1), 0, TILE_TALL_PARTS - 1).astype(jnp.int32)
    sector_across_start = set_ends(jax.random.randint(part_keys[3], (CELL_TOTAL_SUM,), 0, TILE_WIDE_PARTS), jax.random.fold_in(part_keys[3], 1), 0, TILE_WIDE_PARTS - 1).astype(jnp.int32)
    return {"radar_subimages": radar_subimages, "owning_sector": owning_sector, "sector_down_start": sector_down_start, "sector_across_start": sector_across_start}


EPSILON = 1e-06

def box_sum(fields):
    row_total = fields.shape[1]
    col_total = fields.shape[2]
    row_out = row_total // 4
    col_out = col_total // 4
    padded = jnp.pad(fields, ((0, 0), (2, 2), (12, 12)))
    col_sums = sum((padded[:, :, shift_index:shift_index + 4 * col_out:4] for shift_index in range(28)))
    row_sums = sum((col_sums[:, 1 + shift_index:1 + shift_index + 4 * row_out:4, :] for shift_index in range(7)))
    return row_sums

def reference(radar_subimages, owning_sector, sector_down_start, sector_across_start):
    sector_entry_label = owning_sector[:, 0] * SLOTS + sector_down_start * TILE_WIDE_PARTS + sector_across_start
    entry_capacity = N_GRID * SLOTS
    sector_entry_accrual = jax.ops.segment_sum(radar_subimages.astype(jnp.float32), sector_entry_label, num_segments=entry_capacity)
    counts = jax.ops.segment_sum(jnp.ones_like(sector_entry_label), sector_entry_label, num_segments=entry_capacity)
    merged_image = sector_entry_accrual / jnp.maximum(counts, 1).astype(jnp.float32)[:, None, None, None, None]
    merged_image = merged_image.reshape(N_GRID, TILE_TALL_PARTS, TILE_WIDE_PARTS, VISIT_TIMES, 2, CELL_PIXEL_SPAN, CELL_PIXEL_SPAN)
    merged_image = merged_image.transpose(3, 4, 0, 1, 5, 2, 6).reshape(VISIT_TIMES, 2, N_GRID * TILE_TALL_PARTS * CELL_PIXEL_SPAN, TILE_WIDE_PARTS * CELL_PIXEL_SPAN)
    real_part = merged_image[:, 0]
    imag_part = merged_image[:, 1]
    cross_re = real_part[:-1] * real_part[1:] + imag_part[:-1] * imag_part[1:]
    cross_im = imag_part[:-1] * real_part[1:] - real_part[:-1] * imag_part[1:]
    powers = real_part * real_part + imag_part * imag_part
    fields = jnp.concatenate([cross_re, cross_im, powers], 0)
    box_sums = box_sum(fields)
    couple_tally_value = VISIT_TIMES - 1
    magnitude = jnp.sqrt(box_sums[:couple_tally_value] ** 2 + box_sums[couple_tally_value:2 * couple_tally_value] ** 2)
    scale_root = jnp.sqrt(box_sums[2 * couple_tally_value:3 * couple_tally_value] * box_sums[2 * couple_tally_value + 1:] + EPSILON)
    return magnitude / scale_root
```

```python
import functools

import jax
import jax.numpy as jnp
from jax import lax
from jax.experimental import pallas as pl
from jax.experimental.pallas import tpu as pltpu
from jax.sharding import PartitionSpec as P

SUBIMAGE_BOUND = 2
TILE_TALL_PARTS = 4
TILE_WIDE_PARTS = 8
LOOK = 4

EPSILON = 1e-06
MIB = 1 << 20
MESH = pl.DeviceIdType.MESH


def exchange_kernel(
    group,
    owner_ref,
    down_ref,
    across_ref,
    blocks_ref,
    arrived_ref,
    slots_ref,
    staged,
    notes,
    send_sem,
    recv_sem,
    note_send_sem,
    note_recv_sem,
    own_sem,
):
    me = lax.axis_index("grid")
    held = blocks_ref.shape[0]
    lane = lax.broadcasted_iota(jnp.int32, notes.shape[1:], 1)

    def stage(t):
        first, second = jnp.int32(0), jnp.int32(0)
        first_slot, second_slot = jnp.int32(-1), jnp.int32(-1)
        found = jnp.int32(0)
        for b in range(held):
            hit = owner_ref[b] == t
            slot = down_ref[b] * TILE_WIDE_PARTS + across_ref[b]
            take_first = jnp.logical_and(hit, found == 0)
            take_second = jnp.logical_and(hit, found != 0)
            first = jnp.where(take_first, b, first)
            first_slot = jnp.where(take_first, slot, first_slot)
            second = jnp.where(take_second, b, second)
            second_slot = jnp.where(take_second, slot, second_slot)
            found = jnp.where(hit, 1, found)
        staged[t, 0] = blocks_ref[first]
        staged[t, 1] = blocks_ref[second]
        notes[t] = jnp.where(lane == 0, first_slot, jnp.where(lane == 1, second_slot, -1))

    def copies(k):
        t = lax.rem(me + k, group)
        return (
            pltpu.make_async_remote_copy(
                src_ref=staged.at[t],
                dst_ref=arrived_ref.at[me],
                send_sem=send_sem.at[k],
                recv_sem=recv_sem.at[k],
                device_id={"grid": t},
                device_id_type=MESH,
            ),
            pltpu.make_async_remote_copy(
                src_ref=notes.at[t],
                dst_ref=slots_ref.at[me],
                send_sem=note_send_sem.at[k],
                recv_sem=note_recv_sem.at[k],
                device_id={"grid": t},
                device_id_type=MESH,
            ),
        )

    barrier = pltpu.get_barrier_semaphore()

    def greet(k, _):
        pl.semaphore_signal(
            barrier, inc=1, device_id={"grid": lax.rem(me + k, group)}, device_id_type=MESH
        )
        return 0

    lax.fori_loop(1, group, greet, 0)
    pl.semaphore_wait(barrier, group - 1)

    def send(k, _):
        stage(lax.rem(me + k, group))
        block, note = copies(k)
        block.start()
        note.start()
        return 0

    lax.fori_loop(1, group, send, 0)
    stage(me)
    own = (
        pltpu.make_async_copy(staged.at[me], arrived_ref.at[me], own_sem.at[0]),
        pltpu.make_async_copy(notes.at[me], slots_ref.at[me], own_sem.at[1]),
    )
    for copy in own:
        copy.start()

    def finish(k, _):
        for copy in copies(k):
            copy.wait()
        return 0

    lax.fori_loop(1, group, finish, 0)
    for copy in own:
        copy.wait()


def exchange(blocks, owner, down, across):
    group = lax.axis_size("grid")
    held, rows, side = blocks.shape
    staged_bytes = group * SUBIMAGE_BOUND * rows * side * 2
    return pl.pallas_call(
        functools.partial(exchange_kernel, group),
        out_shape=(
            jax.ShapeDtypeStruct((group, SUBIMAGE_BOUND, rows, side), blocks.dtype),
            jax.ShapeDtypeStruct((group, 8, side), jnp.int32),
        ),
        in_specs=[pl.BlockSpec(memory_space=pltpu.SMEM)] * 3
        + [pl.BlockSpec(memory_space=pltpu.VMEM)],
        out_specs=(pl.BlockSpec(memory_space=pl.ANY), pl.BlockSpec(memory_space=pl.ANY)),
        scratch_shapes=[
            pltpu.VMEM((group, SUBIMAGE_BOUND, rows, side), blocks.dtype),
            pltpu.VMEM((group, 8, side), jnp.int32),
            pltpu.SemaphoreType.DMA((group,)),
            pltpu.SemaphoreType.DMA((group,)),
            pltpu.SemaphoreType.DMA((group,)),
            pltpu.SemaphoreType.DMA((group,)),
            pltpu.SemaphoreType.DMA((2,)),
        ],
        compiler_params=pltpu.CompilerParams(
            collective_id=0,
            has_side_effects=True,
            vmem_limit_bytes=staged_bytes + held * rows * side * 2 + 6 * MIB,
        ),
    )(owner, down, across, blocks)


def split_dot(values, table):
    total = None
    rest = values
    for _ in range(3):
        part = rest.astype(jnp.bfloat16)
        rest = rest - part.astype(jnp.float32)
        term = jnp.dot(part, table, preferred_element_type=jnp.float32)
        total = term if total is None else total + term
    return total


def looks_kernel(
    dates, side, slots_ref, arrived_ref, box_ref, edge_ref, image, mid, up, low, edges, table, head, following, amount
):
    slot_total = TILE_TALL_PARTS * TILE_WIDE_PARTS
    lanes = arrived_ref.shape[0]
    channels = 2 * dates
    pairs = dates - 1
    fields = 2 * pairs + dates
    width = TILE_WIDE_PARTS * side
    looks_down = side // LOOK
    rows_out = TILE_TALL_PARTS * looks_down

    def clear(s, _):
        head[s] = -1
        amount[s] = 0
        return 0

    lax.fori_loop(0, slot_total, clear, 0)

    def link(n, _):
        s = slots_ref[n]

        @pl.when(s >= 0)
        def _():
            following[n] = head[s]
            head[s] = n
            amount[s] = amount[s] + 1

        return 0

    lax.fori_loop(0, lanes, link, 0)

    col = lax.broadcasted_iota(jnp.int32, table.shape, 0)
    out = lax.broadcasted_iota(jnp.int32, table.shape, 1)
    table[...] = jnp.where(
        jnp.logical_and(col >= LOOK * out - 12, col <= LOOK * out + 15), 1.0, 0.0
    ).astype(table.dtype)
    up[:, rows_out:, :] = jnp.zeros((fields, 8, width), jnp.float32)
    low[:, :8, :] = jnp.zeros((fields, 8, width), jnp.float32)

    def block_row(r, _):
        for c in range(TILE_WIDE_PARTS):
            s = r * TILE_WIDE_PARTS + c
            first = head[s]
            place = slice(c * channels * side, (c + 1) * channels * side)

            @pl.when(first < 0)
            def _():
                image[place] = jnp.zeros((channels * side, side), jnp.float32)

            @pl.when(first >= 0)
            def _():
                count = jnp.full((8, side), amount[s], jnp.int32).astype(jnp.float32)
                scale = (1.0 / count)[:1]
                image[place] = arrived_ref[first].astype(jnp.float32) * scale

                def more(n):
                    image[place] += arrived_ref[n].astype(jnp.float32) * scale
                    return following[n]

                lax.while_loop(lambda n: n >= 0, more, following[first])

        def chunk(i, _):
            c = i // (looks_down // 8)
            rows = lax.rem(i, looks_down // 8) * 8
            columns = pl.ds(pl.multiple_of(c * side, side), side)
            own, above, below = None, None, None
            for phase in range(LOOK):
                values = [
                    image[pl.ds((c * channels + ch) * side + rows * LOOK + phase, 8, stride=LOOK), :]
                    for ch in range(channels)
                ]
                re, im = values[0::2], values[1::2]
                now = (
                    [re[k] * re[k + 1] + im[k] * im[k + 1] for k in range(pairs)]
                    + [im[k] * re[k + 1] - re[k] * im[k + 1] for k in range(pairs)]
                    + [re[d] * re[d] + im[d] * im[d] for d in range(dates)]
                )
                own = now if phase == 0 else [a + b for a, b in zip(own, now)]
                if phase == 1:
                    above = own
                if phase == LOOK - 1:
                    below = now
            at = r * looks_down + rows
            for f in range(fields):
                mid[f, pl.ds(pl.multiple_of(at, 8), 8), columns] = own[f]
                up[f, pl.ds(pl.multiple_of(at, 8), 8), columns] = above[f]
                low[f, pl.ds(pl.multiple_of(at + 8, 8), 8), columns] = below[f]
            return 0

        lax.fori_loop(0, TILE_WIDE_PARTS * (looks_down // 8), chunk, 0)
        return 0

    lax.fori_loop(0, TILE_TALL_PARTS, block_row, 0)

    def columns_pass(f, _):
        total = mid[f] + up[f, 1 : rows_out + 1, :] + low[f, 7 : rows_out + 7, :]
        box_ref[f] = split_dot(total, table[...])
        return 0

    lax.fori_loop(0, fields, columns_pass, 0)
    edges[...] = jnp.zeros_like(edges)
    for f in range(fields):
        edges[f : f + 1] = up[f, 0:1, :]
        edges[16 + f : 17 + f] = low[f, rows_out + 7 : rows_out + 8, :]
    edge_ref[...] = split_dot(edges[...], table[...])


def looks(slots, arrived, dates):
    lanes, rows, side = arrived.shape
    fields = 3 * dates - 2
    width = TILE_WIDE_PARTS * side
    rows_out = TILE_TALL_PARTS * side // LOOK
    cols_out = width // LOOK
    slot_total = TILE_TALL_PARTS * TILE_WIDE_PARTS
    return pl.pallas_call(
        functools.partial(looks_kernel, dates, side),
        out_shape=(
            jax.ShapeDtypeStruct((fields, rows_out, cols_out), jnp.float32),
            jax.ShapeDtypeStruct((32, cols_out), jnp.float32),
        ),
        in_specs=[
            pl.BlockSpec(memory_space=pltpu.SMEM),
            pl.BlockSpec(memory_space=pltpu.VMEM),
        ],
        out_specs=(pl.BlockSpec(memory_space=pltpu.VMEM), pl.BlockSpec(memory_space=pltpu.VMEM)),
        scratch_shapes=[
            pltpu.VMEM((TILE_WIDE_PARTS * rows, side), jnp.float32),
            pltpu.VMEM((fields, rows_out, width), jnp.float32),
            pltpu.VMEM((fields, rows_out + 8, width), jnp.float32),
            pltpu.VMEM((fields, rows_out + 8, width), jnp.float32),
            pltpu.VMEM((32, width), jnp.float32),
            pltpu.VMEM((width, cols_out), jnp.bfloat16),
            pltpu.SMEM((slot_total,), jnp.int32),
            pltpu.SMEM((lanes,), jnp.int32),
            pltpu.SMEM((slot_total,), jnp.int32),
        ],
        compiler_params=pltpu.CompilerParams(vmem_limit_bytes=58 * MIB),
    )(slots, arrived)


def local(radar_subimages, owning_sector, sector_down_start, sector_across_start):
    held, dates, parts, side, _ = radar_subimages.shape
    blocks = radar_subimages.reshape(held, dates * parts * side, side)
    arrived, notes = exchange(
        blocks, owning_sector[:, 0], sector_down_start, sector_across_start
    )
    slots = notes[:, 0, :SUBIMAGE_BOUND].reshape(-1)
    box, edge = looks(slots, arrived.reshape(-1, dates * parts * side, side), dates)
    count = lax.axis_size("grid")
    fields = box.shape[0]
    after = lax.ppermute(edge[:fields], "grid", [(i + 1, i) for i in range(count - 1)])
    before = lax.ppermute(edge[16 : 16 + fields], "grid", [(i, i + 1) for i in range(count - 1)])
    row = lax.broadcasted_iota(jnp.int32, box.shape, 1)
    box = box + jnp.where(row == 0, before[:, None, :], 0.0)
    box = box + jnp.where(row == box.shape[1] - 1, after[:, None, :], 0.0)
    pairs = dates - 1
    magnitude = jnp.sqrt(box[:pairs] ** 2 + box[pairs : 2 * pairs] ** 2)
    scale_root = jnp.sqrt(box[2 * pairs : 3 * pairs] * box[2 * pairs + 1 :] + EPSILON)
    return magnitude / scale_root


def solution(mesh):
    in_specs = (
        P(("region", "grid"), None, None, None, None),
        P(("region", "grid"), None),
        P(("region", "grid")),
        P(("region", "grid")),
    )
    out_specs = P(None, ("region", "grid"), None)
    return jax.shard_map(local, mesh=mesh, in_specs=in_specs, out_specs=out_specs, check_vma=False)
```

```python
import functools

import jax
import jax.numpy as jnp
from jax import lax
from jax.experimental import pallas as pl
from jax.experimental.pallas import tpu as pltpu
from jax.sharding import PartitionSpec as P

SUBIMAGE_BOUND = 2
TILE_TALL_PARTS = 4
TILE_WIDE_PARTS = 8
LOOK = 4
BAND = 32

EPSILON = 1e-06
MIB = 1 << 20
MESH = pl.DeviceIdType.MESH


def split_dot(values, table):
    total = None
    rest = values
    for _ in range(3):
        part = rest.astype(jnp.bfloat16)
        rest = rest - part.astype(jnp.float32)
        term = jnp.dot(part, table, preferred_element_type=jnp.float32)
        total = term if total is None else total + term
    return total


def looks_kernel(
    group,
    dates,
    owner_ref,
    down_ref,
    across_ref,
    blocks_ref,
    box_ref,
    staged,
    landed,
    notes,
    landed_notes,
    slots,
    chain,
    last,
    amount,
    sums,
    image,
    lines,
    table,
    send_sem,
    recv_sem,
    note_send_sem,
    note_recv_sem,
    own_sem,
):
    me = lax.axis_index("grid")
    held = blocks_ref.shape[0]
    side = blocks_ref.shape[-1]
    bands = side // BAND
    channels = 2 * dates
    pairs = dates - 1
    fields = 2 * pairs + dates
    lanes = group * SUBIMAGE_BOUND
    slot_total = TILE_TALL_PARTS * TILE_WIDE_PARTS
    tall = BAND // LOOK
    lane = lax.broadcasted_iota(jnp.int32, notes.shape[1:], 1)

    def stage(t):
        first, second = jnp.int32(0), jnp.int32(0)
        first_slot, second_slot = jnp.int32(-1), jnp.int32(-1)
        found = jnp.int32(0)
        for b in range(held):
            hit = owner_ref[b] == t
            slot = down_ref[b] * TILE_WIDE_PARTS + across_ref[b]
            take_first = jnp.logical_and(hit, found == 0)
            take_second = jnp.logical_and(hit, found != 0)
            first = jnp.where(take_first, b, first)
            first_slot = jnp.where(take_first, slot, first_slot)
            second = jnp.where(take_second, b, second)
            second_slot = jnp.where(take_second, slot, second_slot)
            found = jnp.where(hit, 1, found)
        staged[t, 0] = blocks_ref[first]
        staged[t, 1] = blocks_ref[second]
        notes[t] = jnp.where(lane == 0, first_slot, jnp.where(lane == 1, second_slot, -1))

    def band_of(t, q):
        return staged.at[t, :, :, pl.ds(q * BAND, BAND), :]

    def band_copy(q, k):
        t = lax.rem(me + k, group)
        return pltpu.make_async_remote_copy(
            src_ref=band_of(t, q),
            dst_ref=landed[q].at[me],
            send_sem=send_sem.at[q, k],
            recv_sem=recv_sem.at[q, k],
            device_id={"grid": t},
            device_id_type=MESH,
        )

    def note_copy(k):
        t = lax.rem(me + k, group)
        return pltpu.make_async_remote_copy(
            src_ref=notes.at[t],
            dst_ref=landed_notes.at[me],
            send_sem=note_send_sem.at[k],
            recv_sem=note_recv_sem.at[k],
            device_id={"grid": t},
            device_id_type=MESH,
        )

    barrier = pltpu.get_barrier_semaphore()

    def greet(k, _):
        pl.semaphore_signal(
            barrier, inc=1, device_id={"grid": lax.rem(me + k, group)}, device_id_type=MESH
        )
        return 0

    lax.fori_loop(1, group, greet, 0)
    pl.semaphore_wait(barrier, group - 1)

    def send_first(k, _):
        stage(lax.rem(me + k, group))
        note_copy(k).start()
        band_copy(0, k).start()
        return 0

    lax.fori_loop(1, group, send_first, 0)
    for q in range(1, bands):

        def send(k, _):
            band_copy(q, k).start()
            return 0

        lax.fori_loop(1, group, send, 0)

    stage(me)
    own = [
        pltpu.make_async_copy(band_of(me, q), landed[q].at[me], own_sem.at[q]) for q in range(bands)
    ]
    own.append(pltpu.make_async_copy(notes.at[me], landed_notes.at[me], own_sem.at[bands]))
    for copy in own:
        copy.start()

    col = lax.broadcasted_iota(jnp.int32, table.shape, 0)
    out = lax.broadcasted_iota(jnp.int32, table.shape, 1)
    table[...] = jnp.where(
        jnp.logical_and(col >= LOOK * out - 12, col <= LOOK * out + 15), 1.0, 0.0
    ).astype(table.dtype)
    sums[lanes] = jnp.zeros(sums.shape[1:], jnp.float32)

    def hear(k, _):
        note_copy(k).wait()
        return 0

    lax.fori_loop(1, group, hear, 0)
    own[bands].wait()
    to_scalars = pltpu.make_async_copy(landed_notes, slots, own_sem.at[bands + 1])
    to_scalars.start()
    to_scalars.wait()

    def link(g, _):
        for j in range(SUBIMAGE_BOUND):
            mine, n = slots[g, 0, j], g * SUBIMAGE_BOUND + j

            def look(h, found):
                for i in range(SUBIMAGE_BOUND):
                    m = h * SUBIMAGE_BOUND + i
                    hit = jnp.logical_and(slots[h, 0, i] == mine, m < n)
                    found = jnp.where(hit, m, found)
                return found

            chain[n] = lax.fori_loop(0, group, look, jnp.int32(lanes))
        return 0

    lax.fori_loop(0, group, link, 0)

    def settle(s, _):
        def look(h, carry):
            found, count = carry
            for i in range(SUBIMAGE_BOUND):
                hit = slots[h, 0, i] == s
                found = jnp.where(hit, h * SUBIMAGE_BOUND + i, found)
                count = jnp.where(hit, count + 1, count)
            return found, count

        found, count = lax.fori_loop(0, group, look, (jnp.int32(lanes), jnp.int32(0)))
        last[s] = found
        amount[s] = jnp.maximum(count, 1)
        return 0

    lax.fori_loop(0, slot_total, settle, 0)
    row = lax.broadcasted_iota(jnp.int32, (tall, side), 0)
    edge_base = fields * TILE_TALL_PARTS
    edge_groups = pl.cdiv(2 * fields, tall)
    lines[edge_base:] = jnp.zeros((TILE_TALL_PARTS * edge_groups,) + lines.shape[1:], jnp.float32)

    for q in range(bands):

        def arrive(k, _):
            band_copy(q, k).wait_recv()
            return 0

        lax.fori_loop(1, group, arrive, 0)
        own[q].wait()

        def add(g, _):
            for j in range(SUBIMAGE_BOUND):
                n = g * SUBIMAGE_BOUND + j
                block = landed[q][g, j].astype(jnp.float32).reshape(sums.shape[1:])
                sums[n] = block + sums[chain[n]]
            return 0

        lax.fori_loop(0, group, add, 0)

        def block_row(r, _):
            for c in range(TILE_WIDE_PARTS):
                s = r * TILE_WIDE_PARTS + c
                count = jnp.full((8, side), amount[s], jnp.int32).astype(jnp.float32)
                scale = (1.0 / count)[:1]
                image[c * channels * BAND : (c + 1) * channels * BAND] = sums[last[s]] * scale
            for c in range(TILE_WIDE_PARTS):
                columns = slice(c * side, (c + 1) * side)
                own_sum, above, below = None, None, None
                for phase in range(LOOK):
                    values = [
                        image[pl.ds((c * channels + ch) * BAND + phase, tall, stride=LOOK), :]
                        for ch in range(channels)
                    ]
                    re, im = values[0::2], values[1::2]
                    now = (
                        [re[k] * re[k + 1] + im[k] * im[k + 1] for k in range(pairs)]
                        + [im[k] * re[k + 1] - re[k] * im[k + 1] for k in range(pairs)]
                        + [re[d] * re[d] + im[d] * im[d] for d in range(dates)]
                    )
                    own_sum = now if phase == 0 else [a + b for a, b in zip(own_sum, now)]
                    if phase == 1:
                        above = own_sum
                    if phase == LOOK - 1:
                        below = now
                for f in range(fields):
                    lines[f * TILE_TALL_PARTS + r, :, columns] = (
                        own_sum[f]
                        + jnp.where(row < tall - 1, pltpu.roll(above[f], tall - 1, 0), 0.0)
                        + jnp.where(row > 0, pltpu.roll(below[f], 1, 0), 0.0)
                    )
                    edge = edge_base + r * edge_groups
                    e = fields + f
                    lines[edge + f // tall, f % tall : f % tall + 1, columns] = above[f][:1]
                    lines[edge + e // tall, e % tall : e % tall + 1, columns] = below[f][tall - 1 :]
            return 0

        lax.fori_loop(0, TILE_TALL_PARTS, block_row, 0)
        box_ref[q] = split_dot(lines[...].reshape(-1, lines.shape[-1]), table[...])

    for q in range(bands):

        def sent(k, _):
            band_copy(q, k).wait_send()
            return 0

        lax.fori_loop(1, group, sent, 0)


def looks(blocks, owner, down, across):
    group = lax.axis_size("grid")
    held, channels, side, _ = blocks.shape
    dates = channels // 2
    lanes = group * SUBIMAGE_BOUND
    bands = side // BAND
    slot_total = TILE_TALL_PARTS * TILE_WIDE_PARTS
    fields = 3 * dates - 2
    width = TILE_WIDE_PARTS * side
    tall = BAND // LOOK
    groups = TILE_TALL_PARTS * (fields + pl.cdiv(2 * fields, tall))
    return pl.pallas_call(
        functools.partial(looks_kernel, group, dates),
        out_shape=jax.ShapeDtypeStruct((bands, groups * tall, width // LOOK), jnp.float32),
        in_specs=[pl.BlockSpec(memory_space=pltpu.SMEM)] * 3
        + [pl.BlockSpec(memory_space=pltpu.VMEM)],
        out_specs=pl.BlockSpec(memory_space=pltpu.VMEM),
        scratch_shapes=[
            pltpu.VMEM((group, SUBIMAGE_BOUND, channels, side, side), blocks.dtype),
            tuple(
                pltpu.VMEM((group, SUBIMAGE_BOUND, channels, BAND, side), blocks.dtype)
                for _ in range(bands)
            ),
            pltpu.VMEM((group, 8, side), jnp.int32),
            pltpu.VMEM((group, 8, side), jnp.int32),
            pltpu.SMEM((group, 8, side), jnp.int32),
            pltpu.SMEM((lanes,), jnp.int32),
            pltpu.SMEM((slot_total,), jnp.int32),
            pltpu.SMEM((slot_total,), jnp.int32),
            pltpu.VMEM((lanes + 1, channels * BAND, side), jnp.float32),
            pltpu.VMEM((TILE_WIDE_PARTS * channels * BAND, side), jnp.float32),
            pltpu.VMEM((groups, tall, width), jnp.float32),
            pltpu.VMEM((width, width // LOOK), jnp.bfloat16),
            pltpu.SemaphoreType.DMA((bands, group)),
            pltpu.SemaphoreType.DMA((bands, group)),
            pltpu.SemaphoreType.DMA((group,)),
            pltpu.SemaphoreType.DMA((group,)),
            pltpu.SemaphoreType.DMA((bands + 2,)),
        ],
        compiler_params=pltpu.CompilerParams(
            collective_id=0, has_side_effects=True, vmem_limit_bytes=60 * MIB
        ),
    )(owner, down, across, blocks)


def local(radar_subimages, owning_sector, sector_down_start, sector_across_start):
    held, dates, parts, side, _ = radar_subimages.shape
    blocks = radar_subimages.reshape(held, dates * parts, side, side)
    box = looks(blocks, owning_sector[:, 0], sector_down_start, sector_across_start)
    count = lax.axis_size("grid")
    bands, _, cols = box.shape
    pairs = dates - 1
    fields = 2 * pairs + dates
    tall = BAND // LOOK
    steps = TILE_TALL_PARTS * bands
    edge_base = fields * TILE_TALL_PARTS * tall
    edges = box[:, edge_base:].reshape(bands, TILE_TALL_PARTS, -1, cols)[:, :, : 2 * fields]
    edges = edges.transpose(2, 1, 0, 3).reshape(2 * fields, steps, cols)
    above, below = edges[:fields], edges[fields:]
    after = lax.ppermute(above[:, 0], "grid", [(i + 1, i) for i in range(count - 1)])
    before = lax.ppermute(below[:, -1], "grid", [(i, i + 1) for i in range(count - 1)])
    above = jnp.concatenate([above[:, 1:], after[:, None]], 1)[:, :, None]
    below = jnp.concatenate([before[:, None], below[:, :-1]], 1)[:, :, None]
    box = box[:, :edge_base].reshape(bands, fields, TILE_TALL_PARTS, tall, cols)
    box = box.transpose(1, 2, 0, 3, 4).reshape(fields, steps, tall, cols)
    row = lax.broadcasted_iota(jnp.int32, box.shape, 2)
    box = box + jnp.where(row == tall - 1, above, 0.0) + jnp.where(row == 0, below, 0.0)
    magnitude = jnp.sqrt(box[:pairs] ** 2 + box[pairs : 2 * pairs] ** 2)
    scale_root = jnp.sqrt(box[2 * pairs : 3 * pairs] * box[2 * pairs + 1 :] + EPSILON)
    return (magnitude / scale_root).reshape(pairs, steps * tall, cols)


def solution(mesh):
    in_specs = (
        P(("region", "grid"), None, None, None, None),
        P(("region", "grid"), None),
        P(("region", "grid")),
        P(("region", "grid")),
    )
    out_specs = P(None, ("region", "grid"), None)
    return jax.shard_map(local, mesh=mesh, in_specs=in_specs, out_specs=out_specs, check_vma=False)
```

```python
import functools

import jax
import jax.numpy as jnp
from jax import lax
from jax.experimental import pallas as pl
from jax.experimental.pallas import tpu as pltpu
from jax.sharding import PartitionSpec as P

SUBIMAGE_BOUND = 2
TILE_TALL_PARTS = 4
TILE_WIDE_PARTS = 8
LOOK = 4
BAND = 32

EPSILON = 1e-06
MIB = 1 << 20
MESH = pl.DeviceIdType.MESH


def split_dot(values, table):
    total = None
    rest = values
    for _ in range(3):
        part = rest.astype(jnp.bfloat16)
        rest = rest - part.astype(jnp.float32)
        term = jnp.dot(part, table, preferred_element_type=jnp.float32)
        total = term if total is None else total + term
    return total


def looks_kernel(
    group,
    dates,
    owner_ref,
    down_ref,
    across_ref,
    source_ref,
    box_ref,
    blocks_ref,
    staged,
    landed,
    notes,
    landed_notes,
    slots,
    chain,
    last,
    amount,
    sums,
    image,
    lines,
    table,
    send_sem,
    recv_sem,
    note_send_sem,
    note_recv_sem,
    own_sem,
):
    me = lax.axis_index("grid")
    held = blocks_ref.shape[0]
    side = blocks_ref.shape[-1]
    bands = side // BAND
    channels = 2 * dates
    pairs = dates - 1
    fields = 2 * pairs + dates
    lanes = group * SUBIMAGE_BOUND
    slot_total = TILE_TALL_PARTS * TILE_WIDE_PARTS
    tall = BAND // LOOK
    lane = lax.broadcasted_iota(jnp.int32, notes.shape[1:], 1)

    def stage(t):
        first, second = jnp.int32(0), jnp.int32(0)
        first_slot, second_slot = jnp.int32(-1), jnp.int32(-1)
        found = jnp.int32(0)
        for b in range(held):
            hit = owner_ref[b] == t
            slot = down_ref[b] * TILE_WIDE_PARTS + across_ref[b]
            take_first = jnp.logical_and(hit, found == 0)
            take_second = jnp.logical_and(hit, found != 0)
            first = jnp.where(take_first, b, first)
            first_slot = jnp.where(take_first, slot, first_slot)
            second = jnp.where(take_second, b, second)
            second_slot = jnp.where(take_second, slot, second_slot)
            found = jnp.where(hit, 1, found)
        staged[t, 0] = blocks_ref[first]
        staged[t, 1] = blocks_ref[second]
        notes[t] = jnp.where(lane == 0, first_slot, jnp.where(lane == 1, second_slot, -1))

    def band_of(t, q):
        return staged.at[t, :, :, pl.ds(q * BAND, BAND), :]

    def band_copy(q, k):
        t = lax.rem(me + k, group)
        return pltpu.make_async_remote_copy(
            src_ref=band_of(t, q),
            dst_ref=landed[q].at[me],
            send_sem=send_sem.at[q, k],
            recv_sem=recv_sem.at[q, k],
            device_id={"grid": t},
            device_id_type=MESH,
        )

    def note_copy(k):
        t = lax.rem(me + k, group)
        return pltpu.make_async_remote_copy(
            src_ref=notes.at[t],
            dst_ref=landed_notes.at[me],
            send_sem=note_send_sem.at[k],
            recv_sem=note_recv_sem.at[k],
            device_id={"grid": t},
            device_id_type=MESH,
        )

    fetch = pltpu.make_async_copy(source_ref, blocks_ref, own_sem.at[bands + 2])
    fetch.start()
    barrier = pltpu.get_barrier_semaphore()

    def greet(k, _):
        pl.semaphore_signal(
            barrier, inc=1, device_id={"grid": lax.rem(me + k, group)}, device_id_type=MESH
        )
        return 0

    lax.fori_loop(1, group, greet, 0)
    pl.semaphore_wait(barrier, group - 1)
    fetch.wait()

    def send_first(k, _):
        stage(lax.rem(me + k, group))
        note_copy(k).start()
        band_copy(0, k).start()
        return 0

    lax.fori_loop(1, group, send_first, 0)
    for q in range(1, bands):

        def send(k, _):
            band_copy(q, k).start()
            return 0

        lax.fori_loop(1, group, send, 0)

    stage(me)
    own = [
        pltpu.make_async_copy(band_of(me, q), landed[q].at[me], own_sem.at[q]) for q in range(bands)
    ]
    own.append(pltpu.make_async_copy(notes.at[me], landed_notes.at[me], own_sem.at[bands]))
    for copy in own:
        copy.start()

    col = lax.broadcasted_iota(jnp.int32, table.shape, 0)
    out = lax.broadcasted_iota(jnp.int32, table.shape, 1)
    table[...] = jnp.where(
        jnp.logical_and(col >= LOOK * out - 12, col <= LOOK * out + 15), 1.0, 0.0
    ).astype(table.dtype)
    sums[lanes] = jnp.zeros(sums.shape[1:], jnp.float32)

    def hear(k, _):
        note_copy(k).wait()
        return 0

    lax.fori_loop(1, group, hear, 0)
    own[bands].wait()
    to_scalars = pltpu.make_async_copy(landed_notes, slots, own_sem.at[bands + 1])
    to_scalars.start()
    to_scalars.wait()

    def sender(k):
        return lax.rem(me + group - k, group)

    def link(g, _):
        for j in range(SUBIMAGE_BOUND):
            mine, n = slots[sender(g), 0, j], g * SUBIMAGE_BOUND + j

            def look(h, found):
                for i in range(SUBIMAGE_BOUND):
                    m = h * SUBIMAGE_BOUND + i
                    hit = jnp.logical_and(slots[sender(h), 0, i] == mine, m < n)
                    found = jnp.where(hit, m, found)
                return found

            chain[n] = lax.fori_loop(0, group, look, jnp.int32(lanes))
        return 0

    lax.fori_loop(0, group, link, 0)

    def settle(s, _):
        def look(h, carry):
            found, count = carry
            for i in range(SUBIMAGE_BOUND):
                hit = slots[sender(h), 0, i] == s
                found = jnp.where(hit, h * SUBIMAGE_BOUND + i, found)
                count = jnp.where(hit, count + 1, count)
            return found, count

        found, count = lax.fori_loop(0, group, look, (jnp.int32(lanes), jnp.int32(0)))
        last[s] = found
        amount[s] = jnp.maximum(count, 1)
        return 0

    lax.fori_loop(0, slot_total, settle, 0)
    row = lax.broadcasted_iota(jnp.int32, (tall, side), 0)
    edge_base = fields * TILE_TALL_PARTS
    edge_groups = pl.cdiv(2 * fields, tall)
    lines[edge_base:] = jnp.zeros((TILE_TALL_PARTS * edge_groups,) + lines.shape[1:], jnp.float32)

    for q in range(bands):

        def add(k):
            for j in range(SUBIMAGE_BOUND):
                n = k * SUBIMAGE_BOUND + j
                block = landed[q][sender(k), j].astype(jnp.float32).reshape(sums.shape[1:])
                sums[n] = block + sums[chain[n]]

        def arrive(k, _):
            band_copy(q, k).wait_recv()
            add(k)
            return 0

        own[q].wait()
        add(0)
        lax.fori_loop(1, group, arrive, 0)

        def block_row(r, _):
            for c in range(TILE_WIDE_PARTS):
                s = r * TILE_WIDE_PARTS + c
                count = jnp.full((8, side), amount[s], jnp.int32).astype(jnp.float32)
                scale = (1.0 / count)[:1]
                image[c * channels * BAND : (c + 1) * channels * BAND] = sums[last[s]] * scale
            for c in range(TILE_WIDE_PARTS):
                columns = slice(c * side, (c + 1) * side)
                own_sum, above, below = None, None, None
                for phase in range(LOOK):
                    values = [
                        image[pl.ds((c * channels + ch) * BAND + phase, tall, stride=LOOK), :]
                        for ch in range(channels)
                    ]
                    re, im = values[0::2], values[1::2]
                    now = (
                        [re[k] * re[k + 1] + im[k] * im[k + 1] for k in range(pairs)]
                        + [im[k] * re[k + 1] - re[k] * im[k + 1] for k in range(pairs)]
                        + [re[d] * re[d] + im[d] * im[d] for d in range(dates)]
                    )
                    own_sum = now if phase == 0 else [a + b for a, b in zip(own_sum, now)]
                    if phase == 1:
                        above = own_sum
                    if phase == LOOK - 1:
                        below = now
                for f in range(fields):
                    lines[f * TILE_TALL_PARTS + r, :, columns] = (
                        own_sum[f]
                        + jnp.where(row < tall - 1, pltpu.roll(above[f], tall - 1, 0), 0.0)
                        + jnp.where(row > 0, pltpu.roll(below[f], 1, 0), 0.0)
                    )
                    edge = edge_base + r * edge_groups
                    e = fields + f
                    lines[edge + f // tall, f % tall : f % tall + 1, columns] = above[f][:1]
                    lines[edge + e // tall, e % tall : e % tall + 1, columns] = below[f][tall - 1 :]
            return 0

        lax.fori_loop(0, TILE_TALL_PARTS, block_row, 0)
        box_ref[q] = split_dot(lines[...].reshape(-1, lines.shape[-1]), table[...])

    for q in range(bands):

        def sent(k, _):
            band_copy(q, k).wait_send()
            return 0

        lax.fori_loop(1, group, sent, 0)


def looks(blocks, owner, down, across):
    group = lax.axis_size("grid")
    held, channels, side, _ = blocks.shape
    dates = channels // 2
    lanes = group * SUBIMAGE_BOUND
    bands = side // BAND
    slot_total = TILE_TALL_PARTS * TILE_WIDE_PARTS
    fields = 3 * dates - 2
    width = TILE_WIDE_PARTS * side
    tall = BAND // LOOK
    groups = TILE_TALL_PARTS * (fields + pl.cdiv(2 * fields, tall))
    return pl.pallas_call(
        functools.partial(looks_kernel, group, dates),
        out_shape=jax.ShapeDtypeStruct((bands, groups * tall, width // LOOK), jnp.float32),
        in_specs=[pl.BlockSpec(memory_space=pltpu.SMEM)] * 3
        + [pl.BlockSpec(memory_space=pl.ANY)],
        out_specs=pl.BlockSpec(memory_space=pltpu.VMEM),
        scratch_shapes=[
            pltpu.VMEM(blocks.shape, blocks.dtype),
            pltpu.VMEM((group, SUBIMAGE_BOUND, channels, side, side), blocks.dtype),
            tuple(
                pltpu.VMEM((group, SUBIMAGE_BOUND, channels, BAND, side), blocks.dtype)
                for _ in range(bands)
            ),
            pltpu.VMEM((group, 8, side), jnp.int32),
            pltpu.VMEM((group, 8, side), jnp.int32),
            pltpu.SMEM((group, 8, side), jnp.int32),
            pltpu.SMEM((lanes,), jnp.int32),
            pltpu.SMEM((slot_total,), jnp.int32),
            pltpu.SMEM((slot_total,), jnp.int32),
            pltpu.VMEM((lanes + 1, channels * BAND, side), jnp.float32),
            pltpu.VMEM((TILE_WIDE_PARTS * channels * BAND, side), jnp.float32),
            pltpu.VMEM((groups, tall, width), jnp.float32),
            pltpu.VMEM((width, width // LOOK), jnp.bfloat16),
            pltpu.SemaphoreType.DMA((bands, group)),
            pltpu.SemaphoreType.DMA((bands, group)),
            pltpu.SemaphoreType.DMA((group,)),
            pltpu.SemaphoreType.DMA((group,)),
            pltpu.SemaphoreType.DMA((bands + 3,)),
        ],
        compiler_params=pltpu.CompilerParams(
            collective_id=0, has_side_effects=True, vmem_limit_bytes=60 * MIB
        ),
    )(owner, down, across, blocks)


def local(radar_subimages, owning_sector, sector_down_start, sector_across_start):
    held, dates, parts, side, _ = radar_subimages.shape
    blocks = radar_subimages.reshape(held, dates * parts, side, side)
    box = looks(blocks, owning_sector[:, 0], sector_down_start, sector_across_start)
    count = lax.axis_size("grid")
    bands, _, cols = box.shape
    pairs = dates - 1
    fields = 2 * pairs + dates
    tall = BAND // LOOK
    steps = TILE_TALL_PARTS * bands
    edge_base = fields * TILE_TALL_PARTS * tall
    edges = box[:, edge_base:].reshape(bands, TILE_TALL_PARTS, -1, cols)[:, :, : 2 * fields]
    edges = edges.transpose(2, 1, 0, 3).reshape(2 * fields, steps, cols)
    above, below = edges[:fields], edges[fields:]
    after = lax.ppermute(above[:, 0], "grid", [(i + 1, i) for i in range(count - 1)])
    before = lax.ppermute(below[:, -1], "grid", [(i, i + 1) for i in range(count - 1)])
    above = jnp.concatenate([above[:, 1:], after[:, None]], 1)[:, :, None]
    below = jnp.concatenate([before[:, None], below[:, :-1]], 1)[:, :, None]
    box = box[:, :edge_base].reshape(bands, fields, TILE_TALL_PARTS, tall, cols)
    box = box.transpose(1, 2, 0, 3, 4).reshape(fields, steps, tall, cols)
    row = lax.broadcasted_iota(jnp.int32, box.shape, 2)
    box = box + jnp.where(row == tall - 1, above, 0.0) + jnp.where(row == 0, below, 0.0)
    magnitude = jnp.sqrt(box[:pairs] ** 2 + box[pairs : 2 * pairs] ** 2)
    scale_root = jnp.sqrt(box[2 * pairs : 3 * pairs] * box[2 * pairs + 1 :] + EPSILON)
    return (magnitude / scale_root).reshape(pairs, steps * tall, cols)


def solution(mesh):
    in_specs = (
        P(("region", "grid"), None, None, None, None),
        P(("region", "grid"), None),
        P(("region", "grid")),
        P(("region", "grid")),
    )
    out_specs = P(None, ("region", "grid"), None)
    return jax.shard_map(local, mesh=mesh, in_specs=in_specs, out_specs=out_specs, check_vma=False)
```

```python
import functools

import jax
import jax.numpy as jnp
from jax import lax
from jax.experimental import pallas as pl
from jax.experimental.pallas import tpu as pltpu
from jax.sharding import PartitionSpec as P

SUBIMAGE_BOUND = 2
TILE_TALL_PARTS = 4
TILE_WIDE_PARTS = 8
LOOK = 4
BAND = 32

EPSILON = 1e-06
MIB = 1 << 20
MESH = pl.DeviceIdType.MESH


def split_dot(values, table):
    total = None
    rest = values
    for _ in range(2):
        part = rest.astype(jnp.bfloat16)
        rest = rest - part.astype(jnp.float32)
        term = jnp.dot(part, table, preferred_element_type=jnp.float32)
        total = term if total is None else total + term
    return total


def looks_kernel(
    group,
    dates,
    owner_ref,
    down_ref,
    across_ref,
    source_ref,
    box_ref,
    blocks_ref,
    staged,
    landed,
    notes,
    landed_notes,
    slots,
    chain,
    last,
    amount,
    sums,
    image,
    lines,
    table,
    send_sem,
    recv_sem,
    note_send_sem,
    note_recv_sem,
    own_sem,
):
    me = lax.axis_index("grid")
    held = blocks_ref.shape[0]
    side = blocks_ref.shape[-1]
    bands = side // BAND
    channels = 2 * dates
    pairs = dates - 1
    fields = 2 * pairs + dates
    lanes = group * SUBIMAGE_BOUND
    slot_total = TILE_TALL_PARTS * TILE_WIDE_PARTS
    tall = BAND // LOOK
    lane = lax.broadcasted_iota(jnp.int32, notes.shape[1:], 1)

    def stage(t):
        first, second = jnp.int32(0), jnp.int32(0)
        first_slot, second_slot = jnp.int32(-1), jnp.int32(-1)
        found = jnp.int32(0)
        for b in range(held):
            hit = owner_ref[b] == t
            slot = down_ref[b] * TILE_WIDE_PARTS + across_ref[b]
            take_first = jnp.logical_and(hit, found == 0)
            take_second = jnp.logical_and(hit, found != 0)
            first = jnp.where(take_first, b, first)
            first_slot = jnp.where(take_first, slot, first_slot)
            second = jnp.where(take_second, b, second)
            second_slot = jnp.where(take_second, slot, second_slot)
            found = jnp.where(hit, 1, found)
        staged[t, 0] = blocks_ref[first]
        staged[t, 1] = blocks_ref[second]
        notes[t] = jnp.where(lane == 0, first_slot, jnp.where(lane == 1, second_slot, -1))

    def band_of(t, q):
        return staged.at[t, :, :, pl.ds(q * BAND, BAND), :]

    def band_copy(q, k):
        t = lax.rem(me + k, group)
        return pltpu.make_async_remote_copy(
            src_ref=band_of(t, q),
            dst_ref=landed[q].at[me],
            send_sem=send_sem.at[q, k],
            recv_sem=recv_sem.at[q, k],
            device_id={"grid": t},
            device_id_type=MESH,
        )

    def note_copy(k):
        t = lax.rem(me + k, group)
        return pltpu.make_async_remote_copy(
            src_ref=notes.at[t],
            dst_ref=landed_notes.at[me],
            send_sem=note_send_sem.at[k],
            recv_sem=note_recv_sem.at[k],
            device_id={"grid": t},
            device_id_type=MESH,
        )

    fetch = pltpu.make_async_copy(source_ref, blocks_ref, own_sem.at[bands + 2])
    fetch.start()
    barrier = pltpu.get_barrier_semaphore()

    def greet(k, _):
        pl.semaphore_signal(
            barrier, inc=1, device_id={"grid": lax.rem(me + k, group)}, device_id_type=MESH
        )
        return 0

    lax.fori_loop(1, group, greet, 0)
    pl.semaphore_wait(barrier, group - 1)
    fetch.wait()

    def send_first(k, _):
        stage(lax.rem(me + k, group))
        note_copy(k).start()
        band_copy(0, k).start()
        return 0

    lax.fori_loop(1, group, send_first, 0)
    for q in range(1, bands):

        def send(k, _):
            band_copy(q, k).start()
            return 0

        lax.fori_loop(1, group, send, 0)

    stage(me)
    own = [
        pltpu.make_async_copy(band_of(me, q), landed[q].at[me], own_sem.at[q]) for q in range(bands)
    ]
    own.append(pltpu.make_async_copy(notes.at[me], landed_notes.at[me], own_sem.at[bands]))
    for copy in own:
        copy.start()

    col = lax.broadcasted_iota(jnp.int32, table.shape, 0)
    out = lax.broadcasted_iota(jnp.int32, table.shape, 1)
    table[...] = jnp.where(
        jnp.logical_and(col >= LOOK * out - 12, col <= LOOK * out + 15), 1.0, 0.0
    ).astype(table.dtype)
    sums[lanes] = jnp.zeros(sums.shape[1:], jnp.float32)

    def hear(k, _):
        note_copy(k).wait()
        return 0

    lax.fori_loop(1, group, hear, 0)
    own[bands].wait()
    to_scalars = pltpu.make_async_copy(landed_notes, slots, own_sem.at[bands + 1])
    to_scalars.start()
    to_scalars.wait()

    def sender(k):
        return lax.rem(me + group - k, group)

    def link(g, _):
        for j in range(SUBIMAGE_BOUND):
            mine, n = slots[sender(g), 0, j], g * SUBIMAGE_BOUND + j

            def look(h, found):
                for i in range(SUBIMAGE_BOUND):
                    m = h * SUBIMAGE_BOUND + i
                    hit = jnp.logical_and(slots[sender(h), 0, i] == mine, m < n)
                    found = jnp.where(hit, m, found)
                return found

            chain[n] = lax.fori_loop(0, group, look, jnp.int32(lanes))
        return 0

    lax.fori_loop(0, group, link, 0)

    def settle(s, _):
        def look(h, carry):
            found, count = carry
            for i in range(SUBIMAGE_BOUND):
                hit = slots[sender(h), 0, i] == s
                found = jnp.where(hit, h * SUBIMAGE_BOUND + i, found)
                count = jnp.where(hit, count + 1, count)
            return found, count

        found, count = lax.fori_loop(0, group, look, (jnp.int32(lanes), jnp.int32(0)))
        last[s] = found
        amount[s] = jnp.maximum(count, 1)
        return 0

    lax.fori_loop(0, slot_total, settle, 0)
    row = lax.broadcasted_iota(jnp.int32, (tall, side), 0)
    edge_base = fields * TILE_TALL_PARTS
    edge_groups = pl.cdiv(2 * fields, tall)
    lines[edge_base:] = jnp.zeros((TILE_TALL_PARTS * edge_groups,) + lines.shape[1:], jnp.float32)

    for q in range(bands):

        def add(k):
            for j in range(SUBIMAGE_BOUND):
                n = k * SUBIMAGE_BOUND + j
                block = landed[q][sender(k), j].astype(jnp.float32).reshape(sums.shape[1:])
                sums[n] = block + sums[chain[n]]

        def arrive(k, _):
            band_copy(q, k).wait_recv()
            add(k)
            return 0

        own[q].wait()
        add(0)
        lax.fori_loop(1, group, arrive, 0)

        def block_row(r, _):
            for c in range(TILE_WIDE_PARTS):
                s = r * TILE_WIDE_PARTS + c
                count = jnp.full((8, side), amount[s], jnp.int32).astype(jnp.float32)
                scale = (1.0 / count)[:1]
                image[c * channels * BAND : (c + 1) * channels * BAND] = sums[last[s]] * scale
            for c in range(TILE_WIDE_PARTS):
                columns = slice(c * side, (c + 1) * side)
                own_sum, above, below = None, None, None
                for phase in range(LOOK):
                    values = [
                        image[pl.ds((c * channels + ch) * BAND + phase, tall, stride=LOOK), :]
                        for ch in range(channels)
                    ]
                    re, im = values[0::2], values[1::2]
                    now = (
                        [re[k] * re[k + 1] + im[k] * im[k + 1] for k in range(pairs)]
                        + [im[k] * re[k + 1] - re[k] * im[k + 1] for k in range(pairs)]
                        + [re[d] * re[d] + im[d] * im[d] for d in range(dates)]
                    )
                    own_sum = now if phase == 0 else [a + b for a, b in zip(own_sum, now)]
                    if phase == 1:
                        above = own_sum
                    if phase == LOOK - 1:
                        below = now
                for f in range(fields):
                    lines[f * TILE_TALL_PARTS + r, :, columns] = (
                        own_sum[f]
                        + jnp.where(row < tall - 1, pltpu.roll(above[f], tall - 1, 0), 0.0)
                        + jnp.where(row > 0, pltpu.roll(below[f], 1, 0), 0.0)
                    )
                    edge = edge_base + r * edge_groups
                    e = fields + f
                    lines[edge + f // tall, f % tall : f % tall + 1, columns] = above[f][:1]
                    lines[edge + e // tall, e % tall : e % tall + 1, columns] = below[f][tall - 1 :]
            return 0

        lax.fori_loop(0, TILE_TALL_PARTS, block_row, 0)
        box_ref[q] = split_dot(lines[...].reshape(-1, lines.shape[-1]), table[...])

    for q in range(bands):

        def sent(k, _):
            band_copy(q, k).wait_send()
            return 0

        lax.fori_loop(1, group, sent, 0)


def looks(blocks, owner, down, across):
    group = lax.axis_size("grid")
    held, channels, side, _ = blocks.shape
    dates = channels // 2
    lanes = group * SUBIMAGE_BOUND
    bands = side // BAND
    slot_total = TILE_TALL_PARTS * TILE_WIDE_PARTS
    fields = 3 * dates - 2
    width = TILE_WIDE_PARTS * side
    tall = BAND // LOOK
    groups = TILE_TALL_PARTS * (fields + pl.cdiv(2 * fields, tall))
    return pl.pallas_call(
        functools.partial(looks_kernel, group, dates),
        out_shape=jax.ShapeDtypeStruct((bands, groups * tall, width // LOOK), jnp.float32),
        in_specs=[pl.BlockSpec(memory_space=pltpu.SMEM)] * 3
        + [pl.BlockSpec(memory_space=pl.ANY)],
        out_specs=pl.BlockSpec(memory_space=pltpu.VMEM),
        scratch_shapes=[
            pltpu.VMEM(blocks.shape, blocks.dtype),
            pltpu.VMEM((group, SUBIMAGE_BOUND, channels, side, side), blocks.dtype),
            tuple(
                pltpu.VMEM((group, SUBIMAGE_BOUND, channels, BAND, side), blocks.dtype)
                for _ in range(bands)
            ),
            pltpu.VMEM((group, 8, side), jnp.int32),
            pltpu.VMEM((group, 8, side), jnp.int32),
            pltpu.SMEM((group, 8, side), jnp.int32),
            pltpu.SMEM((lanes,), jnp.int32),
            pltpu.SMEM((slot_total,), jnp.int32),
            pltpu.SMEM((slot_total,), jnp.int32),
            pltpu.VMEM((lanes + 1, channels * BAND, side), jnp.float32),
            pltpu.VMEM((TILE_WIDE_PARTS * channels * BAND, side), jnp.float32),
            pltpu.VMEM((groups, tall, width), jnp.float32),
            pltpu.VMEM((width, width // LOOK), jnp.bfloat16),
            pltpu.SemaphoreType.DMA((bands, group)),
            pltpu.SemaphoreType.DMA((bands, group)),
            pltpu.SemaphoreType.DMA((group,)),
            pltpu.SemaphoreType.DMA((group,)),
            pltpu.SemaphoreType.DMA((bands + 3,)),
        ],
        compiler_params=pltpu.CompilerParams(
            collective_id=0, has_side_effects=True, vmem_limit_bytes=60 * MIB
        ),
    )(owner, down, across, blocks)


def local(radar_subimages, owning_sector, sector_down_start, sector_across_start):
    held, dates, parts, side, _ = radar_subimages.shape
    blocks = radar_subimages.reshape(held, dates * parts, side, side)
    box = looks(blocks, owning_sector[:, 0], sector_down_start, sector_across_start)
    count = lax.axis_size("grid")
    bands, _, cols = box.shape
    pairs = dates - 1
    fields = 2 * pairs + dates
    tall = BAND // LOOK
    steps = TILE_TALL_PARTS * bands
    edge_base = fields * TILE_TALL_PARTS * tall
    edges = box[:, edge_base:].reshape(bands, TILE_TALL_PARTS, -1, cols)[:, :, : 2 * fields]
    edges = edges.transpose(2, 1, 0, 3).reshape(2 * fields, steps, cols)
    above, below = edges[:fields], edges[fields:]
    after = lax.ppermute(above[:, 0], "grid", [(i + 1, i) for i in range(count - 1)])
    before = lax.ppermute(below[:, -1], "grid", [(i, i + 1) for i in range(count - 1)])
    above = jnp.concatenate([above[:, 1:], after[:, None]], 1)[:, :, None]
    below = jnp.concatenate([before[:, None], below[:, :-1]], 1)[:, :, None]
    box = box[:, :edge_base].reshape(bands, fields, TILE_TALL_PARTS, tall, cols)
    box = box.transpose(1, 2, 0, 3, 4).reshape(fields, steps, tall, cols)
    row = lax.broadcasted_iota(jnp.int32, box.shape, 2)
    box = box + jnp.where(row == tall - 1, above, 0.0) + jnp.where(row == 0, below, 0.0)
    magnitude = jnp.sqrt(box[:pairs] ** 2 + box[pairs : 2 * pairs] ** 2)
    scale_root = jnp.sqrt(box[2 * pairs : 3 * pairs] * box[2 * pairs + 1 :] + EPSILON)
    return (magnitude / scale_root).reshape(pairs, steps * tall, cols)


def solution(mesh):
    in_specs = (
        P(("region", "grid"), None, None, None, None),
        P(("region", "grid"), None),
        P(("region", "grid")),
        P(("region", "grid")),
    )
    out_specs = P(None, ("region", "grid"), None)
    return jax.shard_map(local, mesh=mesh, in_specs=in_specs, out_specs=out_specs, check_vma=False)
```
